32 devices in a mesh: lat: 4 (over y, x), lon: 8 (over z, core).
Axes of the slice: x: 2, y: 2, z: 4, core: 2. Of those that a mesh axis runs over, the one named last changes fastest.
Arguments:
- base_state: float32 [8, 2, 480, 1024], P(None, None, 'lat', 'lon'), may hold values from -6 to 6
- section_state: float32 [8, 2, 480, 1024], P(None, None, 'lat', 'lon'), may hold values from -6 to 6
- cutoff: int32 [480], replicated, may hold values from 8 to 64, as said below
- filter_mask: int32 [480], replicated, may hold values from 0 to 1, as said below
Outputs:
- new_state: float32 [8, 2, 480, 1024], P(None, None, 'lat', 'lon')
The draws below stay inside these ranges and needn't reach their ends.
Inputs may be any that keep to these rules, and one draw needn't show every extreme that they name: `cutoff`: every value lies in 8 to 64, and 64 occurs in every draw. `filter_mask`: 1 exactly on a run of rows starting at each pole, 0 elsewhere; each run holds 1 to 120 rows, and one of the two runs holds exactly 120.
All inputs are finite; a program needn't handle non-finite values.
Results may differ from the reference program's by a relative error of at most 0.0003.
Values sent between devices are 32-bit elements; how exact they have to be, the bound alone decides.
A program may use at most 64 MiB of HBM per device.

```python
import jax
import jax.numpy as jnp
from jax import lax

F = 8
LEV = 2
KMAX = 64
NLAT = 480
NLON = 1024


def draw_cutoff(key, part):
    first_key, second_key = jax.random.split(jax.random.fold_in(key, 11))
    lowest = max(1, KMAX // 8)
    drawn = jax.random.randint(first_key, (NLAT,), lowest, KMAX + 1)
    where_top = jax.random.randint(second_key, (), 0, NLAT)
    return drawn.at[where_top].set(KMAX).astype(jnp.int32)


def draw_filter_mask(key, part):
    first_key, second_key = jax.random.split(jax.random.fold_in(key, 23))
    quarter_rows = NLAT // 4
    other_width = jax.random.randint(first_key, (), 1, quarter_rows + 1)
    which_pole = jax.random.randint(second_key, (), 0, 2)
    south_width = jnp.where(which_pole == 0, quarter_rows, other_width)
    north_width = jnp.where(which_pole == 0, other_width, quarter_rows)
    row_index = jnp.arange(NLAT, dtype=jnp.int32)
    chosen = (row_index < south_width) | (row_index >= NLAT - north_width)
    return chosen.astype(jnp.int32)


def levels(rng, extent, pieces, low, largest):
    gain = 1.0
    for position, blocks in pieces:
        steps = jax.random.uniform(jax.random.fold_in(jax.random.fold_in(rng, 6), position), (blocks,), jnp.float32, low / len(pieces), largest / len(pieces))
        gain = gain * jnp.repeat(jnp.exp(steps), extent[position] // blocks).reshape((-1,) + (1,) * (len(extent) - 1 - position))
    return gain


def noise(rng, dims, spread, reach, shards=(), kind=jnp.bfloat16):
    entries = spread * jax.random.normal(rng, dims, jnp.float32)
    if shards:
        entries = entries * levels(rng, dims, shards, -0.22, 0.18)
    return jnp.clip(entries, -reach, reach).astype(kind)


def setup_inputs(seed: int = 0) -> dict:
    splits = jax.random.split(jax.random.key(seed), 5)
    base_state = noise(splits[0], (F, LEV, NLAT, NLON), 1.0, 6.0, ((2, 4), (3, 8)), jnp.float32)
    section_state = noise(splits[1], (F, LEV, NLAT, NLON), 1.0, 6.0, ((2, 4), (3, 8)), jnp.float32)
    cutoff = draw_cutoff(jax.random.fold_in(splits[4], 71), 0)
    filter_mask = draw_filter_mask(jax.random.fold_in(splits[4], 71), 0)
    return {"base_state": base_state, "section_state": section_state, "cutoff": cutoff, "filter_mask": filter_mask}


section_weight = 0.4


def interface(padded, along):
    length = padded.shape[along]
    outer_low = lax.slice_in_dim(padded, 0, length - 3, axis=along)
    inner_low = lax.slice_in_dim(padded, 1, length - 2, axis=along)
    inner_high = lax.slice_in_dim(padded, 2, length - 1, axis=along)
    outer_high = lax.slice_in_dim(padded, 3, length, axis=along)
    return (7.0 * (inner_low + inner_high) - (outer_low + outer_high)) / 12.0


def cell_cosine(first_row, row_count, total_rows):
    index_rows = first_row + jnp.arange(row_count, dtype=jnp.int32)
    return jnp.sin(jnp.pi * (index_rows.astype(jnp.float32) + 0.5) / total_rows)


def face_cosine(first_row, row_count, total_rows):
    index_faces = first_row + jnp.arange(row_count + 1, dtype=jnp.int32)
    raw_values = jnp.sin(jnp.pi * index_faces.astype(jnp.float32) / total_rows)
    return jnp.where((index_faces == 0) | (index_faces == total_rows), 0.0, raw_values)


def pad_rows(field, flip_sign):
    total_rows = field.shape[1]
    half_cols = field.shape[2] // 2
    padded = jnp.pad(field, ((0, 0), (2, 2), (0, 0)))
    south_row = flip_sign * jnp.roll(field[:, 0], half_cols, axis=-1)
    north_row = flip_sign * jnp.roll(field[:, -1], half_cols, axis=-1)
    return padded.at[:, 1].set(south_row).at[:, total_rows + 2].set(north_row)


def pad_cols(field):
    return jnp.concatenate([field[..., -2:], field, field[..., :2]], axis=-1)


def reference(base_state, section_state, cutoff, filter_mask):
    face_cos = face_cosine(0, NLAT, NLAT)
    cell_cos = cell_cosine(0, NLAT, NLAT)
    u_faces = interface(pad_cols(section_state[0]), 2)
    v_faces = interface(pad_rows(section_state[1], -1.0), 1)
    kept_modes = jnp.arange(NLON // 2 + 1, dtype=jnp.int32)[None, :] < cutoff[:, None]
    rows_kept = filter_mask[:, None] == 1

    def per_field(field_index):
        field = lax.dynamic_index_in_dim(section_state, field_index, 0, keepdims=False)
        flip_sign = jnp.where(field_index < 2, -1.0, 1.0).astype(section_state.dtype)
        north_flux = v_faces * interface(pad_rows(field, flip_sign), 1) * face_cos[None, :, None]
        east_flux = u_faces * interface(pad_cols(field), 2)
        tendency = -((east_flux[..., 1:] - east_flux[..., :-1]) + (north_flux[:, 1:] - north_flux[:, :-1])) / cell_cos[None, :, None]
        spectrum = jnp.fft.rfft(tendency, axis=-1)
        smooth = jnp.fft.irfft(spectrum * kept_modes[None], n=NLON, axis=-1).astype(tendency.dtype)
        filtered = jnp.where(rows_kept[None], smooth, tendency)
        starting = lax.dynamic_index_in_dim(base_state, field_index, 0, keepdims=False)
        return starting + section_weight * filtered

    return lax.map(per_field, jnp.arange(F, dtype=jnp.int32))
```

```python
import functools

import jax
import jax.numpy as jnp
import ml_dtypes
import numpy as np
from jax import lax
from jax.experimental import pallas as pl
from jax.experimental.pallas import tpu as pltpu
from jax.sharding import PartitionSpec as P

KMAX = 64
MODES = 2 * KMAX
LANES = 128
section_weight = 0.4
MESH = pl.DeviceIdType.MESH


def split_halves(table):
    high = table.astype(ml_dtypes.bfloat16)
    low = (table - high.astype(np.float64)).astype(ml_dtypes.bfloat16)
    return high, low


def basis_tables(lon_count, cols):
    total = lon_count * cols
    phase = (np.arange(total)[:, None] * np.arange(KMAX)[None, :]) % total * (2.0 * np.pi / total)
    basis = np.concatenate([np.cos(phase), np.sin(phase)], axis=1).reshape(lon_count, cols, MODES)
    high, low = split_halves(basis)
    wide = np.concatenate([high, low], axis=2)
    forward = np.concatenate([wide, wide], axis=1)
    tall = np.concatenate([high.transpose(0, 2, 1), low.transpose(0, 2, 1)], axis=2)
    inverse = np.concatenate([tall, tall], axis=1)
    return forward, inverse


def geometry_table(lat_count, rows, cols):
    total = lat_count * rows
    faces = np.arange(lat_count)[:, None] * rows + np.arange(rows + 8)[None, :]
    face = np.where((faces == 0) | (faces >= total), 0.0, np.sin(np.pi * faces / total))
    cell = -1.0 / (144.0 * np.sin(np.pi * (np.minimum(faces, total - 1) + 0.5) / total))
    both = np.stack([face, cell], axis=1).astype(np.float32)
    return np.ascontiguousarray(np.broadcast_to(both[..., None], both.shape + (cols,)))


def two_parts(value):
    high = value.astype(jnp.bfloat16)
    low = (value - high.astype(jnp.float32)).astype(jnp.bfloat16)
    return jnp.concatenate([high, low], axis=1)


def kernel(dims, base_hbm, sec_hbm, cut_ref, mask_ref, fwd_hbm, inv_hbm, geo_hbm, out_ref,
           pad, base, fwd, inv, geo, wts, msk, rowpack, halo, colpack, colrecv, comb, ul, ur, vf,
           tend, msend, mrecv, zsend, zrecv, coef,
           lsem, hs_sem, hr_sem, ms_sem, mr_sem, zs_sem, zr_sem, cs_sem, cr_sem, fs_sem):
    F, L, R, C, NLAT, NLON = dims
    S = F * L
    G = NLON // 2
    FG = F // G
    quarter = -(-NLAT // 4)
    band = lax.axis_index("lat")
    lon = lax.axis_index("lon")
    core = lax.rem(lon, 2)
    g = lon // 2
    mate = g * 2 + 1 - core
    polar = (band < quarter) | (band >= NLAT - quarter)

    locals_ = [
        pltpu.make_async_copy(sec_hbm, pad.at[:, pl.ds(8, R), :], lsem.at[0]),
        pltpu.make_async_copy(base_hbm, base, lsem.at[1]),
        pltpu.make_async_copy(fwd_hbm.at[lon], fwd, lsem.at[2]),
        pltpu.make_async_copy(inv_hbm.at[lon], inv, lsem.at[3]),
        pltpu.make_async_copy(geo_hbm.at[band], geo, lsem.at[4]),
    ]
    for copy in locals_:
        copy.start()

    left = lax.rem(lon + NLON - 1, NLON)
    right = lax.rem(lon + 1, NLON)
    cross = lax.rem(lon + NLON // 2, NLON)
    south, north = band == 0, band == NLAT - 1
    lo_dst = (jnp.where(south, 0, band - 1), jnp.where(south, cross, lon))
    hi_dst = (jnp.where(north, band, band + 1), jnp.where(north, cross, lon))
    lo_slot = jnp.where(south, 0, 1)
    hi_slot = jnp.where(north, 1, 0)

    def peer(d):
        return lax.rem(g + d, G)

    barrier = pltpu.get_barrier_semaphore()
    for target in ((band, left), (band, right), lo_dst, hi_dst):
        pl.semaphore_signal(barrier, inc=1, device_id=target, device_id_type=MESH)

    @pl.when(polar)
    def _():
        for d in range(1, G):
            pl.semaphore_signal(
                barrier, inc=1, device_id=(band, peer(d) * 2 + core), device_id_type=MESH
            )

    locals_[0].wait()
    lane = lax.broadcasted_iota(jnp.int32, (R, LANES), 1)
    packed = jnp.zeros((R, LANES), jnp.float32)
    for s in range(S):
        rowpack[0, 2 * s : 2 * s + 2] = pad[s, 8:10]
        rowpack[1, 2 * s : 2 * s + 2] = pad[s, R + 6 : R + 8]
        edge = pad[s, 8 : R + 8, 0:LANES]
        if C > LANES:
            edge = jnp.where(lane < LANES // 2, edge, pad[s, 8 : R + 8, C - LANES : C])
        shifted = pltpu.roll(edge, (4 * s + 2) % LANES, 1)
        packed = jnp.where((lane >= 4 * s) & (lane < 4 * s + 4), shifted, packed)
    colpack[...] = packed

    pl.semaphore_wait(barrier, jnp.where(polar, G + 3, 4))

    def remote(src, dst, send, recv, target):
        return pltpu.make_async_remote_copy(
            src_ref=src, dst_ref=dst, send_sem=send, recv_sem=recv, device_id=target, device_id_type=MESH
        )

    halos = [
        remote(colpack, colrecv.at[0], hs_sem.at[0], hr_sem.at[0], (band, right)),
        remote(colpack, colrecv.at[1], hs_sem.at[1], hr_sem.at[1], (band, left)),
        remote(rowpack.at[0], halo.at[lo_slot], hs_sem.at[2], hr_sem.at[2 + lo_slot], lo_dst),
        remote(rowpack.at[1], halo.at[hi_slot], hs_sem.at[3], hr_sem.at[2 + hi_slot], hi_dst),
    ]
    for copy in halos:
        copy.start()

    @pl.when(polar)
    def _():
        mode = lax.rem(lax.broadcasted_iota(jnp.int32, (1, MODES), 1), KMAX)
        scale = jnp.where(mode == 0, 1.0 / (C * NLON), 2.0 / (C * NLON)).astype(jnp.float32)

        def row(r, carry):
            wts[pl.ds(r, 1), :] = jnp.where(mode < cut_ref[band * R + r], scale, 0.0)
            msk[pl.ds(r, 1), :] = jnp.broadcast_to(mask_ref[band * R + r], (1, C))
            return carry

        lax.fori_loop(0, R, row, 0)

    for copy in locals_[1:]:
        copy.wait()
    for slot in range(2):
        remote(colpack, colrecv.at[slot], hs_sem.at[slot], hr_sem.at[slot], (band, right)).wait_recv()
        remote(
            rowpack.at[slot], halo.at[slot], hs_sem.at[2 + slot], hr_sem.at[2 + slot], (band, right)
        ).wait_recv()

    comb[...] = jnp.where(lax.rem(lane, 4) < 2, colrecv[0], colrecv[1])
    index = lax.broadcasted_iota(jnp.int32, (2 * S, C), 0)
    sign = jnp.where(index < 4 * L, -1.0, 1.0)
    low, high = halo[0], halo[1]
    over_low = jnp.where(lax.rem(index, 2) == 1, sign * pltpu.roll(low, 1, 0), 0.0)
    over_high = jnp.where(lax.rem(index, 2) == 0, sign * pltpu.roll(high, 2 * S - 1, 0), 0.0)
    low = jnp.where(south, over_low, low)
    high = jnp.where(north, over_high, high)
    for s in range(S):
        pad[s, 6:8] = low[2 * s : 2 * s + 2]
        pad[s, R + 8 : R + 10] = high[2 * s : 2 * s + 2]

    wide = lax.broadcasted_iota(jnp.int32, (R, C), 1)

    def east(s):
        x = pad[s, 8 : R + 8]
        e = pltpu.roll(comb[...], lax.rem(2 * LANES - 2 - 4 * s, LANES), 1)
        if C > LANES:
            e = jnp.concatenate([e] * (C // LANES), axis=1)
        m1 = pltpu.roll(jnp.where(wide == C - 1, e, x), 1, 1)
        m2 = pltpu.roll(jnp.where(wide >= C - 2, e, x), 2, 1)
        p1 = pltpu.roll(jnp.where(wide == 0, e, x), C - 1, 1)
        p2 = pltpu.roll(jnp.where(wide < 2, e, x), C - 2, 1)
        return 7.0 * (m1 + x) - (m2 + p1), 7.0 * (x + p1) - (m1 + p2)

    def northward(s):
        return 7.0 * (pad[s, 7 : R + 15] + pad[s, 8 : R + 16]) - (pad[s, 6 : R + 14] + pad[s, 9 : R + 17])

    def winds(l):
        ul[...], ur[...] = east(l)
        vf[...] = northward(L + l) * geo[0]

    def tendency(s):
        wl, wr = east(s)
        fn = vf[...] * northward(s)
        up = pltpu.roll(fn, R + 7, 0)
        return ((ur[...] * wr - ul[...] * wl) + (up[:R] - fn[:R])) * geo[1, :R]

    @pl.when(jnp.logical_not(polar))
    def _():
        def level(l, carry):
            winds(l)

            def field(f, inner):
                s = f * L + l
                out_ref[s] = base[s] + section_weight * tendency(s)
                return inner

            return lax.fori_loop(0, F, field, carry)

        lax.fori_loop(0, L, level, 0)

    @pl.when(polar)
    def _():
        here, other = core, 1 - core

        def order(k):
            return lax.rem((g + 1) * FG + k, F)

        def partial_sums(f, l):
            s = f * L + l
            t = tendency(s)
            tend[s] = t
            both = jnp.dot(two_parts(t), fwd[...], preferred_element_type=jnp.float32)
            return both[:, :MODES] + both[:, MODES:]

        def to_mate(f):
            return remote(msend.at[f], mrecv.at[f], ms_sem.at[f], mr_sem.at[f], (band, mate))

        def to_owner(f):
            slot = lax.rem(f, FG)
            return remote(
                zsend.at[f], zrecv.at[g * FG + slot], zs_sem.at[f], zr_sem.at[g * FG + slot],
                (band, (f // FG) * 2 + core),
            )

        def to_peer(f, d):
            at = here * F + f
            return remote(
                coef.at[at], coef.at[at], cs_sem.at[lax.rem(f, FG) * G + d], cr_sem.at[at],
                (band, peer(d) * 2 + core),
            )

        def forward(f):
            at = here * F + f
            return remote(coef.at[at], coef.at[at], fs_sem.at[f], cr_sem.at[at], (band, mate))

        def arrived(at):
            return remote(coef.at[at], coef.at[at], fs_sem.at[0], cr_sem.at[at], (band, mate))

        def finish(f, l):
            s = f * L + l
            both = jnp.dot(two_parts(coef[l * F + f]), inv[...], preferred_element_type=jnp.float32)
            smooth = both[:, :C] + both[:, C:]
            filtered = jnp.where(msk[...] == 1, smooth, tend[s])
            out_ref[s] = base[s] + section_weight * filtered

        winds(other)

        def stage_a(k, carry):
            f = order(k)
            msend[f] = partial_sums(f, other)
            to_mate(f).start()
            return carry

        lax.fori_loop(0, F, stage_a, 0)
        winds(here)

        def stage_b(k, carry):
            f = order(k)
            mine = partial_sums(f, here)
            to_mate(f).wait_recv()
            zsend[f] = mine + mrecv[f]

            @pl.when(k < F - FG)
            def _():
                to_owner(f).start()

            return carry

        lax.fori_loop(0, F, stage_b, 0)

        def stage_c(j, carry):
            f = g * FG + j
            total = zsend[f]
            for d in range(1, G):
                at = peer(d) * FG + j
                remote(zsend.at[f], zrecv.at[at], zs_sem.at[f], zr_sem.at[at], (band, mate)).wait_recv()
                total = total + zrecv[at]
            coef[here * F + f] = total * wts[...]
            for d in range(1, G):
                to_peer(f, d).start()
            forward(f).start()
            return carry

        lax.fori_loop(0, FG, stage_c, 0)

        def own(j, carry):
            finish(g * FG + j, here)
            return carry

        lax.fori_loop(0, FG, own, 0)

        def stage_d(k, carry):
            f = order(k)
            arrived(here * F + f).wait_recv()
            forward(f).start()
            finish(f, here)
            return carry

        lax.fori_loop(0, F - FG, stage_d, 0)

        def stage_e(k, carry):
            f = lax.rem(g * FG + k, F)
            arrived(other * F + f).wait_recv()
            finish(f, other)
            return carry

        lax.fori_loop(0, F, stage_e, 0)

        def drain(k, carry):
            f = order(k)
            to_mate(f).wait_send()
            forward(f).wait_send()

            @pl.when(k < F - FG)
            def _():
                to_owner(f).wait_send()

            return carry

        lax.fori_loop(0, F, drain, 0)

        def drain_peers(j, carry):
            for d in range(1, G):
                to_peer(g * FG + j, d).wait_send()
            return carry

        lax.fori_loop(0, FG, drain_peers, 0)

    for copy in halos:
        copy.wait_send()


def local(base_state, section_state, cutoff, filter_mask):
    F, L, R, C = section_state.shape
    NLAT, NLON = lax.axis_size("lat"), lax.axis_size("lon")
    S, G = F * L, NLON // 2
    FG = F // G
    forward, inverse = basis_tables(NLON, C)
    geometry = geometry_table(NLAT, R, C)
    f32 = jnp.float32
    sem = pltpu.SemaphoreType.DMA
    hbm = pl.BlockSpec(memory_space=pl.ANY)
    smem = pl.BlockSpec(memory_space=pltpu.SMEM)
    result = pl.pallas_call(
        functools.partial(kernel, (F, L, R, C, NLAT, NLON)),
        out_shape=jax.ShapeDtypeStruct((S, R, C), f32),
        in_specs=[hbm, hbm, smem, smem, hbm, hbm, hbm],
        out_specs=pl.BlockSpec(memory_space=pltpu.VMEM),
        scratch_shapes=[
            pltpu.VMEM((S, R + 24, C), f32),
            pltpu.VMEM((S, R, C), f32),
            pltpu.VMEM((2 * C, 2 * MODES), jnp.bfloat16),
            pltpu.VMEM((2 * MODES, 2 * C), jnp.bfloat16),
            pltpu.VMEM((2, R + 8, C), f32),
            pltpu.VMEM((R, MODES), f32),
            pltpu.VMEM((R, C), jnp.int32),
            pltpu.VMEM((2, 2 * S, C), f32),
            pltpu.VMEM((2, 2 * S, C), f32),
            pltpu.VMEM((R, LANES), f32),
            pltpu.VMEM((2, R, LANES), f32),
            pltpu.VMEM((R, LANES), f32),
            pltpu.VMEM((R, C), f32),
            pltpu.VMEM((R, C), f32),
            pltpu.VMEM((R + 8, C), f32),
            pltpu.VMEM((S, R, C), f32),
            pltpu.VMEM((F, R, MODES), f32),
            pltpu.VMEM((F, R, MODES), f32),
            pltpu.VMEM((F, R, MODES), f32),
            pltpu.VMEM((F, R, MODES), f32),
            pltpu.VMEM((S, R, MODES), f32),
            sem((5,)), sem((4,)), sem((4,)), sem((F,)), sem((F,)), sem((F,)), sem((F,)),
            sem((FG * G,)), sem((S,)), sem((F,)),
        ],
        compiler_params=pltpu.CompilerParams(
            collective_id=0, has_side_effects=True, vmem_limit_bytes=56 * 1024 * 1024
        ),
    )(
        base_state.reshape(S, R, C), section_state.reshape(S, R, C), cutoff, filter_mask,
        jnp.asarray(forward), jnp.asarray(inverse), jnp.asarray(geometry),
    )
    return result.reshape(F, L, R, C)


def solution(mesh):
    placed = (P(None, None, "lat", "lon"), P(None, None, "lat", "lon"), P(), P())
    return jax.shard_map(
        local, mesh=mesh, in_specs=placed, out_specs=P(None, None, "lat", "lon"), check_vma=False
    )
```

```python
import functools

import jax
import jax.numpy as jnp
import ml_dtypes
import numpy as np
from jax import lax
from jax.experimental import pallas as pl
from jax.experimental.pallas import tpu as pltpu
from jax.sharding import PartitionSpec as P

KMAX = 64
MODES = 2 * KMAX
LANES = 128
section_weight = 0.4
MESH = pl.DeviceIdType.MESH


def split_halves(table):
    high = table.astype(ml_dtypes.bfloat16)
    low = (table - high.astype(np.float64)).astype(ml_dtypes.bfloat16)
    return high, low


def basis_tables(lon_count, cols):
    total = lon_count * cols
    phase = (np.arange(total)[:, None] * np.arange(KMAX)[None, :]) % total * (2.0 * np.pi / total)
    basis = np.concatenate([np.cos(phase), np.sin(phase)], axis=1).reshape(lon_count, cols, MODES)
    high, low = split_halves(basis)
    wide = np.concatenate([high, low], axis=2)
    forward = np.concatenate([wide, wide], axis=1)
    tall = np.concatenate([high.transpose(0, 2, 1), low.transpose(0, 2, 1)], axis=2)
    inverse = np.concatenate([tall, tall], axis=1)
    return forward, inverse


def geometry_table(lat_count, rows, cols):
    total = lat_count * rows
    faces = np.arange(lat_count)[:, None] * rows + np.arange(rows + 8)[None, :]
    face = np.where((faces == 0) | (faces >= total), 0.0, np.sin(np.pi * faces / total))
    cell = -1.0 / (144.0 * np.sin(np.pi * (np.minimum(faces, total - 1) + 0.5) / total))
    both = np.stack([face, cell], axis=1).astype(np.float32)
    return np.ascontiguousarray(np.broadcast_to(both[..., None], both.shape + (cols,)))


def two_parts(value):
    high = value.astype(jnp.bfloat16)
    low = (value - high.astype(jnp.float32)).astype(jnp.bfloat16)
    return jnp.concatenate([high, low], axis=1)


def kernel(dims, sec_hbm, cut_ref, mask_ref, fwd_hbm, inv_hbm, geo_hbm, out_ref,
           pad, fwd, inv, geo, wts, msk, rowpack, halo, colpack, colrecv, comb, ul, ur, vf,
           tend, msend, mrecv, zsend, zrecv, coef,
           lsem, hs_sem, hr_sem, ms_sem, mr_sem, zs_sem, zr_sem, cs_sem, cr_sem, fs_sem):
    F, L, R, C, NLAT, NLON, H, RH = dims
    S = F * L
    G = NLON // 2
    U = F * H
    UG = U // G
    half = G // 2
    quarter = -(-NLAT // 4)
    band = lax.axis_index("lat")
    lon = lax.axis_index("lon")
    core = lax.rem(lon, 2)
    g = lon // 2
    mate = g * 2 + 1 - core
    polar = (band < quarter) | (band >= NLAT - quarter)

    locals_ = [
        pltpu.make_async_copy(sec_hbm, pad.at[:, pl.ds(8, R), :], lsem.at[0]),
        pltpu.make_async_copy(fwd_hbm.at[lon], fwd, lsem.at[1]),
        pltpu.make_async_copy(inv_hbm.at[lon], inv, lsem.at[2]),
        pltpu.make_async_copy(geo_hbm.at[band], geo, lsem.at[3]),
    ]
    for copy in locals_:
        copy.start()

    left = lax.rem(lon + NLON - 1, NLON)
    right = lax.rem(lon + 1, NLON)
    cross = lax.rem(lon + NLON // 2, NLON)
    south, north = band == 0, band == NLAT - 1
    lo_dst = (jnp.where(south, 0, band - 1), jnp.where(south, cross, lon))
    hi_dst = (jnp.where(north, band, band + 1), jnp.where(north, cross, lon))
    lo_slot = jnp.where(south, 0, 1)
    hi_slot = jnp.where(north, 1, 0)

    side = g // half

    def peer(d):
        i = lax.rem(d, half)
        far = (1 - side) * half + lax.rem(g + i, half)
        near = side * half + lax.rem(g + 1 + i, half)
        return jnp.where(d < half, far, near)

    barrier = pltpu.get_barrier_semaphore()
    for target in ((band, left), (band, right), lo_dst, hi_dst):
        pl.semaphore_signal(barrier, inc=1, device_id=target, device_id_type=MESH)

    @pl.when(polar)
    def _():
        for d in range(G - 1):
            pl.semaphore_signal(
                barrier, inc=1, device_id=(band, peer(d) * 2 + core), device_id_type=MESH
            )

    locals_[0].wait()
    lane = lax.broadcasted_iota(jnp.int32, (R, LANES), 1)
    packed = jnp.zeros((R, LANES), jnp.float32)
    for s in range(S):
        rowpack[0, 2 * s : 2 * s + 2] = pad[s, 8:10]
        rowpack[1, 2 * s : 2 * s + 2] = pad[s, R + 6 : R + 8]
        edge = pad[s, 8 : R + 8, 0:LANES]
        if C > LANES:
            edge = jnp.where(lane < LANES // 2, edge, pad[s, 8 : R + 8, C - LANES : C])
        shifted = pltpu.roll(edge, (4 * s + 2) % LANES, 1)
        packed = jnp.where((lane >= 4 * s) & (lane < 4 * s + 4), shifted, packed)
    colpack[...] = packed

    pl.semaphore_wait(barrier, jnp.where(polar, G + 3, 4))

    def remote(src, dst, send, recv, target):
        return pltpu.make_async_remote_copy(
            src_ref=src, dst_ref=dst, send_sem=send, recv_sem=recv, device_id=target, device_id_type=MESH
        )

    halos = [
        remote(colpack, colrecv.at[0], hs_sem.at[0], hr_sem.at[0], (band, right)),
        remote(colpack, colrecv.at[1], hs_sem.at[1], hr_sem.at[1], (band, left)),
        remote(rowpack.at[0], halo.at[lo_slot], hs_sem.at[2], hr_sem.at[2 + lo_slot], lo_dst),
        remote(rowpack.at[1], halo.at[hi_slot], hs_sem.at[3], hr_sem.at[2 + hi_slot], hi_dst),
    ]
    for copy in halos:
        copy.start()

    @pl.when(polar)
    def _():
        mode = lax.rem(lax.broadcasted_iota(jnp.int32, (1, MODES), 1), KMAX)
        scale = jnp.where(mode == 0, 1.0 / (C * NLON), 2.0 / (C * NLON)).astype(jnp.float32)

        def row(r, carry):
            wts[pl.ds(r, 1), :] = jnp.where(mode < cut_ref[band * R + r], scale, 0.0)
            msk[pl.ds(r, 1), :] = jnp.broadcast_to(mask_ref[band * R + r], (1, C))
            return carry

        lax.fori_loop(0, R, row, 0)

    for copy in locals_[1:]:
        copy.wait()
    for slot in range(2):
        remote(colpack, colrecv.at[slot], hs_sem.at[slot], hr_sem.at[slot], (band, right)).wait_recv()
        remote(
            rowpack.at[slot], halo.at[slot], hs_sem.at[2 + slot], hr_sem.at[2 + slot], (band, right)
        ).wait_recv()

    comb[...] = jnp.where(lax.rem(lane, 4) < 2, colrecv[0], colrecv[1])
    index = lax.broadcasted_iota(jnp.int32, (2 * S, C), 0)
    sign = jnp.where(index < 4 * L, -1.0, 1.0)
    low, high = halo[0], halo[1]
    over_low = jnp.where(lax.rem(index, 2) == 1, sign * pltpu.roll(low, 1, 0), 0.0)
    over_high = jnp.where(lax.rem(index, 2) == 0, sign * pltpu.roll(high, 2 * S - 1, 0), 0.0)
    low = jnp.where(south, over_low, low)
    high = jnp.where(north, over_high, high)
    for s in range(S):
        pad[s, 6:8] = low[2 * s : 2 * s + 2]
        pad[s, R + 8 : R + 10] = high[2 * s : 2 * s + 2]

    wide = lax.broadcasted_iota(jnp.int32, (R, C), 1)

    def east(s):
        x = pad[s, 8 : R + 8]
        e = pltpu.roll(comb[...], lax.rem(2 * LANES - 2 - 4 * s, LANES), 1)
        if C > LANES:
            e = jnp.concatenate([e] * (C // LANES), axis=1)
        m1 = pltpu.roll(jnp.where(wide == C - 1, e, x), 1, 1)
        m2 = pltpu.roll(jnp.where(wide >= C - 2, e, x), 2, 1)
        p1 = pltpu.roll(jnp.where(wide == 0, e, x), C - 1, 1)
        p2 = pltpu.roll(jnp.where(wide < 2, e, x), C - 2, 1)
        return 7.0 * (m1 + x) - (m2 + p1), 7.0 * (x + p1) - (m1 + p2)

    def northward(s):
        return 7.0 * (pad[s, 7 : R + 15] + pad[s, 8 : R + 16]) - (pad[s, 6 : R + 14] + pad[s, 9 : R + 17])

    def winds(l):
        ul[l], ur[l] = east(l)
        vf[l] = northward(L + l) * geo[0]

    def tendency(s, l):
        wl, wr = east(s)
        fn = vf[l] * northward(s)
        up = pltpu.roll(fn, R + 7, 0)
        return ((ur[l] * wr - ul[l] * wl) + (up[:R] - fn[:R])) * geo[1, :R]

    for l in range(L):
        winds(l)

    @pl.when(jnp.logical_not(polar))
    def _():
        def slab(s, carry):
            out_ref[s] = section_weight * tendency(s, lax.rem(s, L))
            return carry

        lax.fori_loop(0, S, slab, 0)

    @pl.when(polar)
    def _():
        here, other = core, 1 - core

        def order(k):
            if H == 1:
                return peer(k // UG) * UG + lax.rem(k, UG)
            return lax.rem(g // (H // UG) + 1 + k, F)

        def rows_of(h):
            return h * RH, min(R, (h + 1) * RH)

        def partial_sums(f, l):
            s = f * L + l
            t = tendency(s, l)
            tend[s] = t
            both = jnp.dot(two_parts(t), fwd[...], preferred_element_type=jnp.float32)
            return both[:, :MODES] + both[:, MODES:]

        def to_mate(f):
            units = pl.ds(f * H, H)
            return remote(
                msend.at[units], mrecv.at[units], ms_sem.at[f], mr_sem.at[f], (band, mate)
            )

        def to_owner(u):
            slot = g * UG + lax.rem(u, UG)
            return remote(
                zsend.at[u], zrecv.at[slot], zs_sem.at[u], zr_sem.at[slot],
                (band, (u // UG) * 2 + core),
            )

        def to_peer(j, d):
            at = here * U + g * UG + j
            return remote(
                coef.at[at], coef.at[at], cs_sem.at[j * G + d], cr_sem.at[at],
                (band, peer(d) * 2 + core),
            )

        def forward(u):
            at = here * U + u
            return remote(coef.at[at], coef.at[at], fs_sem.at[u], cr_sem.at[at], (band, mate))

        def arrived(at):
            return remote(coef.at[at], coef.at[at], fs_sem.at[0], cr_sem.at[at], (band, mate))

        def store(ref, f, value):
            for h in range(H):
                first, last = rows_of(h)
                ref[f * H + h, 0 : last - first] = value[first:last]

        def finish(f, l):
            s = f * L + l
            for h in range(H):
                first, last = rows_of(h)
                c = coef[l * U + f * H + h]
                both = jnp.dot(two_parts(c), inv[...], preferred_element_type=jnp.float32)
                smooth = (both[:, :C] + both[:, C:])[: last - first]
                out_ref[s, first:last] = section_weight * jnp.where(
                    msk[first:last] == 1, smooth, tend[s, first:last]
                )

        def combine(f):
            to_mate(f).wait_recv()
            for h in range(H):
                u = f * H + h
                zsend[u] = zsend[u] + mrecv[u]

                @pl.when(u // UG != g)
                def _():
                    to_owner(u).start()

        if H > 1:
            zsend[...] = jnp.zeros_like(zsend)
            msend[...] = jnp.zeros_like(msend)

        def stage_a(k, carry):
            f = order(k)
            store(msend, f, partial_sums(f, other))
            to_mate(f).start()
            store(zsend, f, partial_sums(f, here))

            @pl.when(k > 0)
            def _():
                combine(order(k - 1))

            return carry

        lax.fori_loop(0, F, stage_a, 0)
        combine(order(F - 1))

        def stage_c(j, carry):
            u = g * UG + j
            total = zsend[u]
            for d in range(G - 1):
                at = peer(d) * UG + j
                remote(zsend.at[u], zrecv.at[at], zs_sem.at[u], zr_sem.at[at], (band, mate)).wait_recv()
                total = total + zrecv[at]
            first = pl.multiple_of(lax.rem(u, H) * RH, 8)
            coef[here * U + u] = total * wts[pl.ds(first, RH), :]
            for d in range(G - 1):
                to_peer(j, d).start()
            forward(u).start()
            return carry

        lax.fori_loop(0, UG, stage_c, 0)

        def finish_other(f):
            for h in range(H):
                arrived(other * U + f * H + h).wait_recv()
            finish(f, other)

        def stage_d(k, carry):
            f = order(F - 1 - k)
            for h in range(H):
                u = f * H + h

                @pl.when(u // UG != g)
                def _():
                    arrived(here * U + u).wait_recv()
                    forward(u).start()

            finish(f, here)

            @pl.when(k > 0)
            def _():
                finish_other(order(F - k))

            return carry

        lax.fori_loop(0, F, stage_d, 0)
        finish_other(order(0))

        def drain(f, carry):
            to_mate(f).wait_send()
            for h in range(H):
                u = f * H + h
                forward(u).wait_send()

                @pl.when(u // UG != g)
                def _():
                    to_owner(u).wait_send()

            return carry

        lax.fori_loop(0, F, drain, 0)

        def drain_peers(j, carry):
            for d in range(G - 1):
                to_peer(j, d).wait_send()
            return carry

        lax.fori_loop(0, UG, drain_peers, 0)

    for copy in halos:
        copy.wait_send()


def local(base_state, section_state, cutoff, filter_mask):
    F, L, R, C = section_state.shape
    NLAT, NLON = lax.axis_size("lat"), lax.axis_size("lon")
    S, G = F * L, NLON // 2
    H = max(1, G // F)
    RH = -(-R // (8 * H)) * 8
    U = F * H
    UG = U // G
    forward, inverse = basis_tables(NLON, C)
    geometry = geometry_table(NLAT, R, C)
    f32 = jnp.float32
    sem = pltpu.SemaphoreType.DMA
    hbm = pl.BlockSpec(memory_space=pltpu.HBM)
    smem = pl.BlockSpec(memory_space=pltpu.SMEM)
    filtered = pl.pallas_call(
        functools.partial(kernel, (F, L, R, C, NLAT, NLON, H, RH)),
        out_shape=jax.ShapeDtypeStruct((S, R, C), f32),
        in_specs=[hbm, smem, smem, hbm, hbm, hbm],
        out_specs=pl.BlockSpec(memory_space=pltpu.VMEM),
        scratch_shapes=[
            pltpu.VMEM((S, R + 24, C), f32),
            pltpu.VMEM((2 * C, 2 * MODES), jnp.bfloat16),
            pltpu.VMEM((2 * MODES, 2 * C), jnp.bfloat16),
            pltpu.VMEM((2, R + 8, C), f32),
            pltpu.VMEM((H * RH, MODES), f32),
            pltpu.VMEM((R, C), jnp.int32),
            pltpu.VMEM((2, 2 * S, C), f32),
            pltpu.VMEM((2, 2 * S, C), f32),
            pltpu.VMEM((R, LANES), f32),
            pltpu.VMEM((2, R, LANES), f32),
            pltpu.VMEM((R, LANES), f32),
            pltpu.VMEM((L, R, C), f32),
            pltpu.VMEM((L, R, C), f32),
            pltpu.VMEM((L, R + 8, C), f32),
            pltpu.VMEM((S, R, C), f32),
            pltpu.VMEM((U, RH, MODES), f32),
            pltpu.VMEM((U, RH, MODES), f32),
            pltpu.VMEM((U, RH, MODES), f32),
            pltpu.VMEM((U, RH, MODES), f32),
            pltpu.VMEM((L * U, RH, MODES), f32),
            sem((4,)), sem((4,)), sem((4,)), sem((F,)), sem((F,)), sem((U,)), sem((U,)),
            sem((UG * G,)), sem((L * U,)), sem((U,)),
        ],
        compiler_params=pltpu.CompilerParams(
            collective_id=0, has_side_effects=True, vmem_limit_bytes=18 * S * R * C * 4
        ),
    )(
        section_state.reshape(S, R, C), cutoff, filter_mask,
        jnp.asarray(forward), jnp.asarray(inverse), jnp.asarray(geometry),
    )
    return base_state + filtered.reshape(F, L, R, C)


def solution(mesh):
    placed = (P(None, None, "lat", "lon"), P(None, None, "lat", "lon"), P(), P())
    return jax.shard_map(
        local, mesh=mesh, in_specs=placed, out_specs=P(None, None, "lat", "lon"), check_vma=False
    )
```

```python
import functools

import jax
import jax.numpy as jnp
import numpy as np
from jax import lax
from jax.experimental import pallas as pl
from jax.experimental.pallas import tpu as pltpu
from jax.sharding import PartitionSpec as P

KMAX = 64
MODES = 2 * KMAX
LANES = 128
section_weight = 0.4
MESH = pl.DeviceIdType.MESH


def basis_table(lon_count, cols):
    total = lon_count * cols
    phase = (np.arange(total)[:, None] * np.arange(KMAX)[None, :]) % total * (2.0 * np.pi / total)
    basis = np.concatenate([np.cos(phase), np.sin(phase)], axis=1).reshape(lon_count, cols, MODES)
    return np.stack([basis, basis.transpose(0, 2, 1)], axis=1).astype(np.float32)


def geometry_table(lat_count, rows, cols):
    total = lat_count * rows
    faces = np.arange(lat_count)[:, None] * rows + np.arange(rows + 8)[None, :]
    face = np.where((faces == 0) | (faces >= total), 0.0, np.sin(np.pi * faces / total))
    cell = -1.0 / (144.0 * np.sin(np.pi * (np.minimum(faces, total - 1) + 0.5) / total))
    both = np.stack([face, cell], axis=1).astype(np.float32)
    return np.broadcast_to(both[..., None], both.shape + (cols,))


def two_parts(value):
    high = value.astype(jnp.bfloat16)
    low = (value - high.astype(jnp.float32)).astype(jnp.bfloat16)
    return jnp.concatenate([high, low], axis=1)


def kernel(dims, sec_hbm, cut_ref, mask_ref, table_hbm, out_ref,
           pad, table, fwd, inv, geo, wts, msk, rowpack, halo, colpack, colrecv, comb, ul, ur, vf,
           tend, msend, mrecv, zsend, zrecv, hrecv, coef,
           lsem, hs_sem, hr_sem, ms_sem, mr_sem, zs_sem, zr_sem, xs_sem, xr_sem,
           cs_sem, cr_sem, fs_sem):
    F, L, R, C, NLAT, NLON, H, RH = dims
    S = F * L
    G = NLON // 2
    U = F * H
    UG = U // (2 * G)
    V = U // 2
    half = G // 2
    quarter = NLAT // 4
    band = lax.axis_index("lat")
    lon = lax.axis_index("lon")
    core = lax.rem(lon, 2)
    g = lon // 2
    mate = g * 2 + 1 - core
    block = band // quarter
    polar = (block == 0) | (block == 3)
    partner = band + quarter * (1 - 2 * lax.rem(block, 2))

    locals_ = [
        pltpu.make_async_copy(sec_hbm, pad.at[:, pl.ds(8, R), :], lsem.at[0]),
        pltpu.make_async_copy(table_hbm.at[lon], table, lsem.at[1]),
        pltpu.make_async_copy(table_hbm.at[NLON + band], geo, lsem.at[2]),
    ]
    for copy in locals_:
        copy.start()

    left = lax.rem(lon + NLON - 1, NLON)
    right = lax.rem(lon + 1, NLON)
    cross = lax.rem(lon + NLON // 2, NLON)
    south, north = band == 0, band == NLAT - 1
    lo_dst = (jnp.where(south, 0, band - 1), jnp.where(south, cross, lon))
    hi_dst = (jnp.where(north, band, band + 1), jnp.where(north, cross, lon))
    lo_slot = jnp.where(south, 0, 1)
    hi_slot = jnp.where(north, 1, 0)

    side = g // half

    def peer(d):
        i = lax.rem(d, half)
        far = (1 - side) * half + lax.rem(g + i, half)
        near = side * half + lax.rem(g + 1 + i, half)
        return jnp.where(d < half, far, near)

    barrier = pltpu.get_barrier_semaphore()
    for target in ((band, left), (band, right), lo_dst, hi_dst):
        pl.semaphore_signal(barrier, inc=1, device_id=target, device_id_type=MESH)

    for d in range(G):
        pl.semaphore_signal(
            barrier, inc=1, device_id=(partner, peer(d) * 2 + core), device_id_type=MESH
        )
        if d < G - 1:
            pl.semaphore_signal(
                barrier, inc=1, device_id=(band, peer(d) * 2 + core), device_id_type=MESH
            )

    locals_[0].wait()
    lane = lax.broadcasted_iota(jnp.int32, (R, LANES), 1)
    packed = jnp.zeros((R, LANES), jnp.float32)
    for s in range(S):
        rowpack[0, 2 * s : 2 * s + 2] = pad[s, 8:10]
        rowpack[1, 2 * s : 2 * s + 2] = pad[s, R + 6 : R + 8]
        edge = pad[s, 8 : R + 8, 0:LANES]
        if C > LANES:
            edge = jnp.where(lane < LANES // 2, edge, pad[s, 8 : R + 8, C - LANES : C])
        shifted = pltpu.roll(edge, (4 * s + 2) % LANES, 1)
        packed = jnp.where((lane >= 4 * s) & (lane < 4 * s + 4), shifted, packed)
    colpack[...] = packed

    pl.semaphore_wait(barrier, 2 * G + 3)

    def remote(src, dst, send, recv, target):
        return pltpu.make_async_remote_copy(
            src_ref=src, dst_ref=dst, send_sem=send, recv_sem=recv, device_id=target, device_id_type=MESH
        )

    halos = [
        remote(colpack, colrecv.at[0], hs_sem.at[0], hr_sem.at[0], (band, right)),
        remote(colpack, colrecv.at[1], hs_sem.at[1], hr_sem.at[1], (band, left)),
        remote(rowpack.at[0], halo.at[lo_slot], hs_sem.at[2], hr_sem.at[2 + lo_slot], lo_dst),
        remote(rowpack.at[1], halo.at[hi_slot], hs_sem.at[3], hr_sem.at[2 + hi_slot], hi_dst),
    ]
    for copy in halos:
        copy.start()

    @pl.when(polar)
    def _():
        mode = lax.rem(lax.broadcasted_iota(jnp.int32, (1, MODES), 1), KMAX)
        scale = jnp.where(mode == 0, 1.0 / (C * NLON), 2.0 / (C * NLON)).astype(jnp.float32)

        def row(r, carry):
            wts[pl.ds(r, 1), :] = jnp.where(mode < cut_ref[band * R + r], scale, 0.0)
            msk[pl.ds(r, 1), :] = jnp.broadcast_to(mask_ref[band * R + r], (1, C))
            return carry

        lax.fori_loop(0, R, row, 0)

    for copy in locals_[1:]:
        copy.wait()
    for slot in range(2):
        remote(colpack, colrecv.at[slot], hs_sem.at[slot], hr_sem.at[slot], (band, right)).wait_recv()
        remote(
            rowpack.at[slot], halo.at[slot], hs_sem.at[2 + slot], hr_sem.at[2 + slot], (band, right)
        ).wait_recv()

    @pl.when(polar)
    def _():
        both = two_parts(table[0, :C, :MODES])
        fwd[...] = jnp.concatenate([both, both], axis=0)
        both = two_parts(table[1, :MODES])
        inv[...] = jnp.concatenate([both, both], axis=0)

    comb[...] = jnp.where(lax.rem(lane, 4) < 2, colrecv[0], colrecv[1])
    index = lax.broadcasted_iota(jnp.int32, (2 * S, C), 0)
    sign = jnp.where(index < 4 * L, -1.0, 1.0)
    low, high = halo[0], halo[1]
    over_low = jnp.where(lax.rem(index, 2) == 1, sign * pltpu.roll(low, 1, 0), 0.0)
    over_high = jnp.where(lax.rem(index, 2) == 0, sign * pltpu.roll(high, 2 * S - 1, 0), 0.0)
    low = jnp.where(south, over_low, low)
    high = jnp.where(north, over_high, high)
    for s in range(S):
        pad[s, 6:8] = low[2 * s : 2 * s + 2]
        pad[s, R + 8 : R + 10] = high[2 * s : 2 * s + 2]

    wide = lax.broadcasted_iota(jnp.int32, (R, C), 1)

    def east(s):
        x = pad[s, 8 : R + 8]
        e = pltpu.roll(comb[...], lax.rem(2 * LANES - 2 - 4 * s, LANES), 1)
        if C > LANES:
            e = jnp.concatenate([e] * (C // LANES), axis=1)
        m1 = pltpu.roll(jnp.where(wide == C - 1, e, x), 1, 1)
        m2 = pltpu.roll(jnp.where(wide >= C - 2, e, x), 2, 1)
        p1 = pltpu.roll(jnp.where(wide == 0, e, x), C - 1, 1)
        p2 = pltpu.roll(jnp.where(wide < 2, e, x), C - 2, 1)
        return 7.0 * (m1 + x) - (m2 + p1), 7.0 * (x + p1) - (m1 + p2)

    def northward(s):
        return 7.0 * (pad[s, 7 : R + 15] + pad[s, 8 : R + 16]) - (pad[s, 6 : R + 14] + pad[s, 9 : R + 17])

    def winds(l):
        ul[l], ur[l] = east(l)
        vf[l] = northward(L + l) * geo[0, : R + 8]

    def tendency(s, l):
        wl, wr = east(s)
        fn = vf[l] * northward(s)
        up = pltpu.roll(fn, R + 7, 0)
        return ((ur[l] * wr - ul[l] * wl) + (up[:R] - fn[:R])) * geo[1, :R]

    for l in range(L):
        winds(l)

    here, other = core, 1 - core

    def order(k):
        i = k // 2
        if H == 1:
            first = peer(i // UG) * UG + lax.rem(i, UG)
        else:
            first = lax.rem(g * UG // H + 1 + i, F // 2)
        return first + (F // 2) * (1 - lax.rem(k, 2))

    def to_helper(u):
        v = u - V
        return remote(
            zsend.at[u], hrecv.at[v], xs_sem.at[v], xr_sem.at[v], (partner, lon)
        )

    def to_owner(ref, v):
        slot = g * UG + lax.rem(v, UG)
        return remote(
            ref.at[v], zrecv.at[slot], zs_sem.at[v], zr_sem.at[slot],
            (band, (v // UG) * 2 + core),
        )

    def gathered(ref, j):
        total = ref[g * UG + j]
        for d in range(G - 1):
            at = peer(d) * UG + j
            remote(
                zsend.at[at], zrecv.at[at], zs_sem.at[at], zr_sem.at[at], (band, mate)
            ).wait_recv()
            total = total + zrecv[at]
        return total

    def publish(u, j, d, row):
        at = here * U + u
        return remote(
            coef.at[at], coef.at[at], cs_sem.at[j * G + d], cr_sem.at[at],
            (row, peer(d) * 2 + core),
        )

    @pl.when(jnp.logical_not(polar))
    def _():
        share = (3 * S) // (4 * (F // 2))

        def slab(s, carry):
            out_ref[s] = section_weight * tendency(s, lax.rem(s, L))
            return carry

        def relay(i, carry):
            lax.fori_loop(i * share, (i + 1) * share, slab, 0)
            f = order(2 * i)
            for h in range(H):
                u = f * H + h
                to_helper(u).wait_recv()

                @pl.when((u - V) // UG != g)
                def _():
                    to_owner(hrecv, u - V).start()

            return carry

        lax.fori_loop(0, F // 2, relay, 0)
        lax.fori_loop(share * (F // 2), S, slab, 0)

        def sums(j, carry):
            u = V + g * UG + j
            coef[here * U + u] = gathered(hrecv, j)
            for d in range(G):
                publish(u, j, d, partner).start()
            return carry

        lax.fori_loop(0, UG, sums, 0)

        def drain(v, carry):
            @pl.when(v // UG != g)
            def _():
                to_owner(hrecv, v).wait_send()

            return carry

        lax.fori_loop(0, V, drain, 0)

        def drain_sums(j, carry):
            for d in range(G):
                publish(V + g * UG + j, j, d, partner).wait_send()
            return carry

        lax.fori_loop(0, UG, drain_sums, 0)

    @pl.when(polar)
    def _():
        def rows_of(h):
            return h * RH, min(R, (h + 1) * RH)

        def partial_sums(f, l):
            s = f * L + l
            t = tendency(s, l)
            tend[s] = t
            both = jnp.dot(two_parts(t), fwd[...], preferred_element_type=jnp.float32)
            return both[:, :MODES] + both[:, MODES:]

        def to_mate(f):
            units = pl.ds(f * H, H)
            return remote(
                msend.at[units], mrecv.at[units], ms_sem.at[f], mr_sem.at[f], (band, mate)
            )

        def forward(u):
            at = here * U + u
            return remote(coef.at[at], coef.at[at], fs_sem.at[u], cr_sem.at[at], (band, mate))

        def arrived(at):
            return remote(coef.at[at], coef.at[at], fs_sem.at[0], cr_sem.at[at], (band, mate))

        def store(ref, f, value):
            for h in range(H):
                first, last = rows_of(h)
                ref[f * H + h, 0 : last - first] = value[first:last]

        def finish(f, l):
            s = f * L + l
            for h in range(H):
                first, last = rows_of(h)
                c = coef[l * U + f * H + h] * wts[h * RH : (h + 1) * RH]
                both = jnp.dot(two_parts(c), inv[...], preferred_element_type=jnp.float32)
                smooth = (both[:, :C] + both[:, C:])[: last - first]
                out_ref[s, first:last] = section_weight * jnp.where(
                    msk[first:last] == 1, smooth, tend[s, first:last]
                )

        def combine(f):
            to_mate(f).wait_recv()
            for h in range(H):
                u = f * H + h
                zsend[u] = zsend[u] + mrecv[u]

                @pl.when(u >= V)
                def _():
                    to_helper(u).start()

                @pl.when((u < V) & (u // UG != g))
                def _():
                    to_owner(zsend, u).start()

        if H > 1:
            zsend[...] = jnp.zeros_like(zsend)
            msend[...] = jnp.zeros_like(msend)

        def stage_a(k, carry):
            f = order(k)
            store(msend, f, partial_sums(f, other))
            to_mate(f).start()
            store(zsend, f, partial_sums(f, here))

            @pl.when(k > 0)
            def _():
                combine(order(k - 1))

            return carry

        lax.fori_loop(0, F, stage_a, 0)
        combine(order(F - 1))

        def stage_c(j, carry):
            u = g * UG + j
            coef[here * U + u] = gathered(zsend, j)
            for d in range(G - 1):
                publish(u, j, d, band).start()
            forward(u).start()
            return carry

        lax.fori_loop(0, UG, stage_c, 0)

        def finish_other(f):
            for h in range(H):
                arrived(other * U + f * H + h).wait_recv()
            finish(f, other)

        def back(k):
            return order(jnp.where(k < F // 2, F - 1 - 2 * k, 2 * F - 2 - 2 * k))

        def stage_d(k, carry):
            f = back(k)
            for h in range(H):
                u = f * H + h

                @pl.when((u >= V) | (u // UG != g))
                def _():
                    arrived(here * U + u).wait_recv()
                    forward(u).start()

            finish(f, here)

            @pl.when(k > 0)
            def _():
                finish_other(back(k - 1))

            return carry

        lax.fori_loop(0, F, stage_d, 0)
        finish_other(back(F - 1))

        def drain(f, carry):
            to_mate(f).wait_send()
            for h in range(H):
                u = f * H + h
                forward(u).wait_send()

                @pl.when(u >= V)
                def _():
                    to_helper(u).wait_send()

                @pl.when((u < V) & (u // UG != g))
                def _():
                    to_owner(zsend, u).wait_send()

            return carry

        lax.fori_loop(0, F, drain, 0)

        def drain_peers(j, carry):
            for d in range(G - 1):
                publish(g * UG + j, j, d, band).wait_send()
            return carry

        lax.fori_loop(0, UG, drain_peers, 0)

    for copy in halos:
        copy.wait_send()


def local(base_state, section_state, cutoff, filter_mask):
    F, L, R, C = section_state.shape
    NLAT, NLON = lax.axis_size("lat"), lax.axis_size("lon")
    S, G = F * L, NLON // 2
    H = max(1, 2 * G // F)
    RH = -(-R // (8 * H)) * 8
    U = F * H
    UG = U // (2 * G)
    bases, geometry = basis_table(NLON, C), geometry_table(NLAT, R, C)
    tall = max(C, MODES, R + 8)
    tables = np.zeros((NLON + NLAT, 2, tall, C), np.float32)
    tables[:NLON, :, :C] = bases
    tables[NLON:, :, : R + 8] = geometry
    f32 = jnp.float32
    sem = pltpu.SemaphoreType.DMA
    hbm = pl.BlockSpec(memory_space=pltpu.HBM)
    smem = pl.BlockSpec(memory_space=pltpu.SMEM)
    filtered = pl.pallas_call(
        functools.partial(kernel, (F, L, R, C, NLAT, NLON, H, RH)),
        out_shape=jax.ShapeDtypeStruct((S, R, C), f32),
        in_specs=[hbm, smem, smem, hbm],
        out_specs=pl.BlockSpec(memory_space=pltpu.VMEM),
        scratch_shapes=[
            pltpu.VMEM((S, R + 24, C), f32),
            pltpu.VMEM((2, tall, C), f32),
            pltpu.VMEM((2 * C, 2 * MODES), jnp.bfloat16),
            pltpu.VMEM((2 * MODES, 2 * C), jnp.bfloat16),
            pltpu.VMEM((2, tall, C), f32),
            pltpu.VMEM((H * RH, MODES), f32),
            pltpu.VMEM((R, C), jnp.int32),
            pltpu.VMEM((2, 2 * S, C), f32),
            pltpu.VMEM((2, 2 * S, C), f32),
            pltpu.VMEM((R, LANES), f32),
            pltpu.VMEM((2, R, LANES), f32),
            pltpu.VMEM((R, LANES), f32),
            pltpu.VMEM((L, R, C), f32),
            pltpu.VMEM((L, R, C), f32),
            pltpu.VMEM((L, R + 8, C), f32),
            pltpu.VMEM((S, R, C), f32),
            pltpu.VMEM((U, RH, MODES), f32),
            pltpu.VMEM((U, RH, MODES), f32),
            pltpu.VMEM((U, RH, MODES), f32),
            pltpu.VMEM((U // 2, RH, MODES), f32),
            pltpu.VMEM((U // 2, RH, MODES), f32),
            pltpu.VMEM((L * U, RH, MODES), f32),
            sem((4,)), sem((4,)), sem((4,)), sem((F,)), sem((F,)), sem((U // 2,)), sem((U // 2,)),
            sem((U // 2,)), sem((U // 2,)),
            sem((UG * G,)), sem((L * U,)), sem((U,)),
        ],
        compiler_params=pltpu.CompilerParams(
            collective_id=0, has_side_effects=True, vmem_limit_bytes=55 * S * R * C * 4
        ),
    )(
        section_state.reshape(S, R, C), cutoff, filter_mask,
        jnp.asarray(tables),
    )
    return base_state + filtered.reshape(F, L, R, C)


def solution(mesh):
    placed = (P(None, None, "lat", "lon"), P(None, None, "lat", "lon"), P(), P())
    return jax.shard_map(
        local, mesh=mesh, in_specs=placed, out_specs=P(None, None, "lat", "lon"), check_vma=False
    )
```

```python
import functools

import jax
import jax.numpy as jnp
import numpy as np
from jax import lax
from jax.experimental import pallas as pl
from jax.experimental.pallas import tpu as pltpu
from jax.sharding import PartitionSpec as P

KMAX = 64
MODES = 2 * KMAX
LANES = 128
section_weight = 0.4
MESH = pl.DeviceIdType.MESH


def basis_table(lon_count, cols):
    total = lon_count * cols
    phase = (np.arange(total)[:, None] * np.arange(KMAX)[None, :]) % total * (2.0 * np.pi / total)
    basis = np.concatenate([np.cos(phase), np.sin(phase)], axis=1).reshape(lon_count, cols, MODES)
    return np.stack([basis, basis.transpose(0, 2, 1)], axis=1).astype(np.float32)


def geometry_table(lat_count, rows, cols):
    total = lat_count * rows
    faces = np.arange(lat_count)[:, None] * rows + np.arange(rows + 8)[None, :]
    face = np.where((faces == 0) | (faces >= total), 0.0, np.sin(np.pi * faces / total))
    cell = -1.0 / (144.0 * np.sin(np.pi * (np.minimum(faces, total - 1) + 0.5) / total))
    both = np.stack([face, cell], axis=1).astype(np.float32)
    return np.broadcast_to(both[..., None], both.shape + (cols,))


def two_parts(value):
    high = value.astype(jnp.bfloat16)
    low = (value - high.astype(jnp.float32)).astype(jnp.bfloat16)
    return jnp.concatenate([high, low], axis=1)


def kernel(dims, sec_hbm, code_ref, table_hbm, out_ref,
           pad, table, fwd, inv, geo, wts, msk, rowpack, halo, colpack, colrecv, comb, ul, ur, vf,
           tend, msend, mrecv, zsend, zrecv, hrecv, coef,
           lsem, hs_sem, hr_sem, ms_sem, mr_sem, zs_sem, zr_sem, xs_sem, xr_sem,
           cs_sem, cr_sem, fs_sem):
    F, L, R, C, NLAT, NLON, H, RH = dims
    S = F * L
    G = NLON // 2
    U = F * H
    UG = U // (2 * G)
    V = U // 2
    half = G // 2
    quarter = NLAT // 4
    band = lax.axis_index("lat")
    lon = lax.axis_index("lon")
    core = lax.rem(lon, 2)
    g = lon // 2
    mate = g * 2 + 1 - core
    block = band // quarter
    polar = (block == 0) | (block == 3)
    partner = band + quarter * (1 - 2 * lax.rem(block, 2))

    locals_ = [
        pltpu.make_async_copy(sec_hbm, pad.at[:, pl.ds(8, R), :], lsem.at[0]),
        pltpu.make_async_copy(table_hbm.at[lon], table, lsem.at[1]),
        pltpu.make_async_copy(table_hbm.at[NLON + band], geo, lsem.at[2]),
    ]
    for copy in locals_:
        copy.start()

    left = lax.rem(lon + NLON - 1, NLON)
    right = lax.rem(lon + 1, NLON)
    cross = lax.rem(lon + NLON // 2, NLON)
    south, north = band == 0, band == NLAT - 1
    lo_dst = (jnp.where(south, 0, band - 1), jnp.where(south, cross, lon))
    hi_dst = (jnp.where(north, band, band + 1), jnp.where(north, cross, lon))
    lo_slot = jnp.where(south, 0, 1)
    hi_slot = jnp.where(north, 1, 0)

    side = g // half

    def peer(d):
        i = lax.rem(d, half)
        far = (1 - side) * half + lax.rem(g + i, half)
        near = side * half + lax.rem(g + 1 + i, half)
        return jnp.where(d < half, far, near)

    barrier = pltpu.get_barrier_semaphore()
    for target in ((band, left), (band, right), lo_dst, hi_dst):
        pl.semaphore_signal(barrier, inc=1, device_id=target, device_id_type=MESH)

    for d in range(G):
        pl.semaphore_signal(
            barrier, inc=1, device_id=(partner, peer(d) * 2 + core), device_id_type=MESH
        )
        if d < G - 1:
            pl.semaphore_signal(
                barrier, inc=1, device_id=(band, peer(d) * 2 + core), device_id_type=MESH
            )

    locals_[0].wait()
    lane = lax.broadcasted_iota(jnp.int32, (R, LANES), 1)
    packed = jnp.zeros((R, LANES), jnp.float32)
    for s in range(S):
        rowpack[0, 2 * s : 2 * s + 2] = pad[s, 8:10]
        rowpack[1, 2 * s : 2 * s + 2] = pad[s, R + 6 : R + 8]
        edge = pad[s, 8 : R + 8, 0:LANES]
        if C > LANES:
            edge = jnp.where(lane < LANES // 2, edge, pad[s, 8 : R + 8, C - LANES : C])
        shifted = pltpu.roll(edge, (4 * s + 2) % LANES, 1)
        packed = jnp.where((lane >= 4 * s) & (lane < 4 * s + 4), shifted, packed)
    colpack[...] = packed

    pl.semaphore_wait(barrier, 2 * G + 3)

    def remote(src, dst, send, recv, target):
        return pltpu.make_async_remote_copy(
            src_ref=src, dst_ref=dst, send_sem=send, recv_sem=recv, device_id=target, device_id_type=MESH
        )

    halos = [
        remote(colpack, colrecv.at[0], hs_sem.at[0], hr_sem.at[0], (band, right)),
        remote(colpack, colrecv.at[1], hs_sem.at[1], hr_sem.at[1], (band, left)),
        remote(rowpack.at[0], halo.at[lo_slot], hs_sem.at[2], hr_sem.at[2 + lo_slot], lo_dst),
        remote(rowpack.at[1], halo.at[hi_slot], hs_sem.at[3], hr_sem.at[2 + hi_slot], hi_dst),
    ]
    for copy in halos:
        copy.start()

    @pl.when(polar)
    def _():
        mode = lax.rem(lax.broadcasted_iota(jnp.int32, (1, MODES), 1), KMAX)
        scale = jnp.where(mode == 0, 1.0 / (C * NLON), 2.0 / (C * NLON)).astype(jnp.float32)

        def row(r, carry):
            code = code_ref[band * R + r]
            wts[pl.ds(r, 1), :] = jnp.where(mode < code // 2, scale, 0.0)
            msk[pl.ds(r, 1), :] = jnp.broadcast_to(lax.rem(code, 2), (1, C))
            return carry

        lax.fori_loop(0, R, row, 0)

    for copy in locals_[1:]:
        copy.wait()
    for slot in range(2):
        remote(colpack, colrecv.at[slot], hs_sem.at[slot], hr_sem.at[slot], (band, right)).wait_recv()
        remote(
            rowpack.at[slot], halo.at[slot], hs_sem.at[2 + slot], hr_sem.at[2 + slot], (band, right)
        ).wait_recv()

    @pl.when(polar)
    def _():
        both = two_parts(table[0, :C, :MODES])
        fwd[...] = jnp.concatenate([both, both], axis=0)
        both = two_parts(table[1, :MODES])
        inv[...] = jnp.concatenate([both, both], axis=0)

    comb[...] = jnp.where(lax.rem(lane, 4) < 2, colrecv[0], colrecv[1])
    index = lax.broadcasted_iota(jnp.int32, (2 * S, C), 0)
    sign = jnp.where(index < 4 * L, -1.0, 1.0)
    low, high = halo[0], halo[1]
    over_low = jnp.where(lax.rem(index, 2) == 1, sign * pltpu.roll(low, 1, 0), 0.0)
    over_high = jnp.where(lax.rem(index, 2) == 0, sign * pltpu.roll(high, 2 * S - 1, 0), 0.0)
    low = jnp.where(south, over_low, low)
    high = jnp.where(north, over_high, high)
    for s in range(S):
        pad[s, 6:8] = low[2 * s : 2 * s + 2]
        pad[s, R + 8 : R + 10] = high[2 * s : 2 * s + 2]

    wide = lax.broadcasted_iota(jnp.int32, (R, C), 1)

    def east(s):
        x = pad[s, 8 : R + 8]
        e = pltpu.roll(comb[...], lax.rem(2 * LANES - 2 - 4 * s, LANES), 1)
        if C > LANES:
            e = jnp.concatenate([e] * (C // LANES), axis=1)
        m1 = pltpu.roll(jnp.where(wide == C - 1, e, x), 1, 1)
        m2 = pltpu.roll(jnp.where(wide >= C - 2, e, x), 2, 1)
        p1 = pltpu.roll(jnp.where(wide == 0, e, x), C - 1, 1)
        p2 = pltpu.roll(jnp.where(wide < 2, e, x), C - 2, 1)
        return 7.0 * (m1 + x) - (m2 + p1), 7.0 * (x + p1) - (m1 + p2)

    def northward(s):
        return 7.0 * (pad[s, 7 : R + 15] + pad[s, 8 : R + 16]) - (pad[s, 6 : R + 14] + pad[s, 9 : R + 17])

    def winds(l):
        ul[l], ur[l] = east(l)
        vf[l] = northward(L + l) * geo[0, : R + 8]

    def tendency(s, l):
        wl, wr = east(s)
        fn = vf[l] * northward(s)
        up = pltpu.roll(fn, R + 7, 0)
        return ((ur[l] * wr - ul[l] * wl) + (up[:R] - fn[:R])) * geo[1, :R]

    for l in range(L):
        winds(l)

    here, other = core, 1 - core

    def order(k):
        i = k // 2
        if UG % H == 0:
            first = peer(i // (UG // H)) * (UG // H) + lax.rem(i, UG // H)
        else:
            first = lax.rem(g * UG // H + 1 + i, F // 2)
        return first + (F // 2) * (1 - lax.rem(k, 2))

    def to_helper(u):
        v = u - V
        return remote(
            zsend.at[u], hrecv.at[v], xs_sem.at[v], xr_sem.at[v], (partner, lon)
        )

    def to_owner(ref, v):
        slot = g * UG + lax.rem(v, UG)
        return remote(
            ref.at[v], zrecv.at[slot], zs_sem.at[v], zr_sem.at[slot],
            (band, (v // UG) * 2 + core),
        )

    def gathered(ref, j):
        total = ref[g * UG + j]
        for d in range(G - 1):
            at = peer(d) * UG + j
            remote(
                zsend.at[at], zrecv.at[at], zs_sem.at[at], zr_sem.at[at], (band, mate)
            ).wait_recv()
            total = total + zrecv[at]
        return total

    def publish(u, j, d, row):
        at = here * U + u
        return remote(
            coef.at[at], coef.at[at], cs_sem.at[j * G + d], cr_sem.at[at],
            (row, peer(d) * 2 + core),
        )

    @pl.when(jnp.logical_not(polar))
    def _():
        share = S // (F // 2)

        def slab(s, carry):
            out_ref[s] = section_weight * tendency(s, lax.rem(s, L))
            return carry

        def relay(i, carry):
            lax.fori_loop(i * share, (i + 1) * share, slab, 0)
            f = order(2 * i)
            for h in range(H):
                u = f * H + h
                to_helper(u).wait_recv()

                @pl.when((u - V) // UG != g)
                def _():
                    to_owner(hrecv, u - V).start()

            return carry

        lax.fori_loop(0, F // 2, relay, 0)
        lax.fori_loop(share * (F // 2), S, slab, 0)

        def sums(j, carry):
            u = V + g * UG + j
            coef[here * U + u] = gathered(hrecv, j)
            for d in range(G):
                publish(u, j, d, partner).start()
            return carry

        lax.fori_loop(0, UG, sums, 0)

        def drain(v, carry):
            @pl.when(v // UG != g)
            def _():
                to_owner(hrecv, v).wait_send()

            return carry

        lax.fori_loop(0, V, drain, 0)

        def drain_sums(j, carry):
            for d in range(G):
                publish(V + g * UG + j, j, d, partner).wait_send()
            return carry

        lax.fori_loop(0, UG, drain_sums, 0)

    @pl.when(polar)
    def _():
        def rows_of(h):
            return h * RH, min(R, (h + 1) * RH)

        def partial_sums(f, l):
            s = f * L + l
            t = tendency(s, l)
            tend[s] = t
            both = jnp.dot(two_parts(t), fwd[...], preferred_element_type=jnp.float32)
            return both[:, :MODES] + both[:, MODES:]

        def to_mate(f):
            units = pl.ds(f * H, H)
            return remote(
                msend.at[units], mrecv.at[units], ms_sem.at[f], mr_sem.at[f], (band, mate)
            )

        def forward(u):
            at = here * U + u
            return remote(coef.at[at], coef.at[at], fs_sem.at[u], cr_sem.at[at], (band, mate))

        def arrived(at):
            return remote(coef.at[at], coef.at[at], fs_sem.at[0], cr_sem.at[at], (band, mate))

        def store(ref, f, value):
            for h in range(H):
                first, last = rows_of(h)
                ref[f * H + h, 0 : last - first] = value[first:last]

        def finish(f, l):
            s = f * L + l
            for h in range(H):
                first, last = rows_of(h)
                c = coef[l * U + f * H + h] * wts[h * RH : (h + 1) * RH]
                both = jnp.dot(two_parts(c), inv[...], preferred_element_type=jnp.float32)
                smooth = (both[:, :C] + both[:, C:])[: last - first]
                out_ref[s, first:last] = section_weight * jnp.where(
                    msk[first:last] == 1, smooth, tend[s, first:last]
                )

        def combine(f):
            to_mate(f).wait_recv()
            for h in range(H):
                u = f * H + h
                zsend[u] = zsend[u] + mrecv[u]

                @pl.when(u >= V)
                def _():
                    to_helper(u).start()

                @pl.when((u < V) & (u // UG != g))
                def _():
                    to_owner(zsend, u).start()

        if H * RH > R:
            zsend[...] = jnp.zeros_like(zsend)
            msend[...] = jnp.zeros_like(msend)

        def stage_a(k, carry):
            f = order(k)
            store(msend, f, partial_sums(f, other))
            to_mate(f).start()
            store(zsend, f, partial_sums(f, here))

            @pl.when(k > 0)
            def _():
                combine(order(k - 1))

            return carry

        lax.fori_loop(0, F, stage_a, 0)
        combine(order(F - 1))

        def stage_c(j, carry):
            u = g * UG + j
            coef[here * U + u] = gathered(zsend, j)
            for d in range(G - 1):
                publish(u, j, d, band).start()
            forward(u).start()
            return carry

        lax.fori_loop(0, UG, stage_c, 0)

        def finish_other(f):
            for h in range(H):
                arrived(other * U + f * H + h).wait_recv()
            finish(f, other)

        def back(k):
            return order(jnp.where(k < F // 2, F - 1 - 2 * k, 2 * F - 2 - 2 * k))

        def stage_d(k, carry):
            f = back(k)
            for h in range(H):
                u = f * H + h

                @pl.when((u >= V) | (u // UG != g))
                def _():
                    arrived(here * U + u).wait_recv()
                    forward(u).start()

            finish(f, here)

            @pl.when(k > 0)
            def _():
                finish_other(back(k - 1))

            return carry

        lax.fori_loop(0, F, stage_d, 0)
        finish_other(back(F - 1))

        def drain(f, carry):
            to_mate(f).wait_send()
            for h in range(H):
                u = f * H + h
                forward(u).wait_send()

                @pl.when(u >= V)
                def _():
                    to_helper(u).wait_send()

                @pl.when((u < V) & (u // UG != g))
                def _():
                    to_owner(zsend, u).wait_send()

            return carry

        lax.fori_loop(0, F, drain, 0)

        def drain_peers(j, carry):
            for d in range(G - 1):
                publish(g * UG + j, j, d, band).wait_send()
            return carry

        lax.fori_loop(0, UG, drain_peers, 0)

    for copy in halos:
        copy.wait_send()


def local(base_state, section_state, cutoff, filter_mask):
    F, L, R, C = section_state.shape
    NLAT, NLON = lax.axis_size("lat"), lax.axis_size("lon")
    S, G = F * L, NLON // 2
    H = max(1, 2 * G // F)
    RH = -(-R // (8 * H)) * 8
    U = F * H
    UG = U // (2 * G)
    bases, geometry = basis_table(NLON, C), geometry_table(NLAT, R, C)
    tall = max(C, MODES, R + 8)
    tables = np.zeros((NLON + NLAT, 2, tall, C), np.float32)
    tables[:NLON, :, :C] = bases
    tables[NLON:, :, : R + 8] = geometry
    f32 = jnp.float32
    sem = pltpu.SemaphoreType.DMA
    hbm = pl.BlockSpec(memory_space=pltpu.HBM)
    smem = pl.BlockSpec(memory_space=pltpu.SMEM)
    filtered = pl.pallas_call(
        functools.partial(kernel, (F, L, R, C, NLAT, NLON, H, RH)),
        out_shape=jax.ShapeDtypeStruct((S, R, C), f32),
        in_specs=[hbm, smem, hbm],
        out_specs=pl.BlockSpec(memory_space=pltpu.VMEM),
        scratch_shapes=[
            pltpu.VMEM((S, R + 24, C), f32),
            pltpu.VMEM((2, tall, C), f32),
            pltpu.VMEM((2 * C, 2 * MODES), jnp.bfloat16),
            pltpu.VMEM((2 * MODES, 2 * C), jnp.bfloat16),
            pltpu.VMEM((2, tall, C), f32),
            pltpu.VMEM((H * RH, MODES), f32),
            pltpu.VMEM((R, C), jnp.int32),
            pltpu.VMEM((2, 2 * S, C), f32),
            pltpu.VMEM((2, 2 * S, C), f32),
            pltpu.VMEM((R, LANES), f32),
            pltpu.VMEM((2, R, LANES), f32),
            pltpu.VMEM((R, LANES), f32),
            pltpu.VMEM((L, R, C), f32),
            pltpu.VMEM((L, R, C), f32),
            pltpu.VMEM((L, R + 8, C), f32),
            pltpu.VMEM((S, R, C), f32),
            pltpu.VMEM((U, RH, MODES), f32),
            pltpu.VMEM((U, RH, MODES), f32),
            pltpu.VMEM((U, RH, MODES), f32),
            pltpu.VMEM((U // 2, RH, MODES), f32),
            pltpu.VMEM((U // 2, RH, MODES), f32),
            pltpu.VMEM((L * U, RH, MODES), f32),
            sem((4,)), sem((4,)), sem((4,)), sem((F,)), sem((F,)), sem((U // 2,)), sem((U // 2,)),
            sem((U // 2,)), sem((U // 2,)),
            sem((UG * G,)), sem((L * U,)), sem((U,)),
        ],
        compiler_params=pltpu.CompilerParams(
            collective_id=0, has_side_effects=True, vmem_limit_bytes=int(56.4 * S * R * C * 4)
        ),
    )(
        section_state.reshape(S, R, C),
        2 * cutoff + jnp.where(filter_mask == 1, 1, 0),
        jnp.asarray(tables),
    )
    return base_state + filtered.reshape(F, L, R, C)


def solution(mesh):
    placed = (P(None, None, "lat", "lon"), P(None, None, "lat", "lon"), P(), P())
    return jax.shard_map(
        local, mesh=mesh, in_specs=placed, out_specs=P(None, None, "lat", "lon"), check_vma=False
    )
```
